32 devices in a mesh: tp: 2 (over x), ep: 16 (over z, y, core).
Axes of the slice: x: 2, y: 2, z: 4, core: 2. Of those that a mesh axis runs over, the one named last changes fastest.
Arguments:
- attn: bfloat16 [8192, 1536], P('ep', 'tp'), may hold values from -6 to 6
- resid: bfloat16 [8192, 1536], P('ep', 'tp'), may hold values from -6 to 6
- w_out: bfloat16 [1536, 1536], P('tp', 'ep'), may hold values from -0.15625 to 0.15625
- gain_mix: float32 [1536], replicated, may hold values from 0.1 to 1.9
- gain_out: float32 [1536], replicated, may hold values from 0.1 to 1.9
- routes: int32 [8192, 8], P('ep'), may hold values from 0 to 39, all different within a row; in each aligned block of 256 rows (0 to 255, 256 to 511, ...) at most 64 rows name the same one
- gates: float32 [8192, 8], P('ep'), may hold values from 0.05 to 1
- w_gate: bfloat16 [48, 1536, 512], P('ep'), as said below
- w_up: bfloat16 [48, 1536, 512], P('ep'), as said below
- w_down: bfloat16 [48, 512, 1536], P('ep'), as said below
Outputs:
- layer_out: bfloat16 [8192, 1536], P('ep', 'tp')
The draws below stay inside these ranges and needn't reach their ends.
Inputs may be any that keep to these rules, and one draw needn't show every extreme that they name: `routes`: in each aligned block of 256 rows no expert is named more than 64 times; each row names 8 different experts. `w_gate`: copy s holds the weights of expert s % 40. `w_up`: copy s holds the weights of expert s % 40. `w_down`: copy s holds the weights of expert s % 40.
All inputs are finite; a program needn't handle non-finite values.
Results may differ from the reference program's by a relative error of at most 0.0053.
Values may be sent and summed in bfloat16 or wider, within the bound.
A program may use at most 128 MiB of HBM per device.

```python
import math
import jax
import jax.numpy as jnp
import numpy as np
from jax import lax

D = 1536
FF = 512
EXPERTS = 40
TOPK = 8
TOKENS = 8192
BLOCK = 256
MOST = 64
SLOTS = 48


def expert_copies(key, shape, fan_in):
    expert_ids = jnp.arange(SLOTS) % EXPERTS

    def one_copy(expert):
        return jax.random.normal(jax.random.fold_in(key, expert), shape, jnp.float32) * fan_in ** (-0.5)
    return jax.vmap(one_copy)(expert_ids).astype(jnp.bfloat16)


def draw_w_gate(key, part):
    return expert_copies(jax.random.fold_in(key, 11), (D, FF), D)


def draw_w_up(key, part):
    return expert_copies(jax.random.fold_in(key, 23), (D, FF), D)


def draw_w_down(key, part):
    return expert_copies(jax.random.fold_in(key, 37), (FF, D), FF)


def shard_levels(key, shape, split, smallest, largest):
    loudness, own = 1.0, jax.random.fold_in(key, 6)
    for axis_at, parts in split:
        draws = jnp.exp(jax.random.uniform(jax.random.fold_in(own, axis_at), (parts,), jnp.float32, smallest / len(split), largest / len(split)))
        loudness = loudness * jnp.repeat(draws, shape[axis_at] // parts).reshape([-1 if axis == axis_at else 1 for axis in range(len(shape))])
    return loudness


def shared_out(own_key, own, number, rows, count, top, limit, lean):
    order = jax.random.permutation(own_key, count)
    crowded, usual = portions_of(count, rows * top, limit, lean, True), portions_of(count, rows * top, limit, lean, False)
    places = jnp.arange(count)

    def named(sizes, turn):
        used = int((sizes > 0).sum())
        fixed = max(1, used // 4)
        shifted = fixed + (places - fixed + turn * (used - fixed)) % max(1, count - fixed)
        return jnp.zeros((count,), jnp.int32).at[order[jnp.where(places < fixed, places, shifted)]].set(jnp.asarray(sizes, jnp.int32))

    sizes = jnp.where(number % 4 == 0, named(crowded, number // 4), named(usual, number - number // 4 - 1))
    mixed = jax.random.permutation(jax.random.fold_in(own, 3), count)
    giver, sink = mixed[0:count // 2 * 2:2], mixed[1:count // 2 * 2:2]
    margin = jnp.minimum(sizes[giver] - 1, limit - sizes[sink]) // 2
    margin = jnp.where((giver == order[0]) | (sink == order[0]) | (sizes[sink] == 0), 0, jnp.maximum(margin, 0))
    shifted = jax.random.randint(jax.random.fold_in(own, 4), (count // 2,), 0, 1 << 20) % (margin + 1)
    sizes = sizes.at[giver].add(-shifted).at[sink].add(shifted)
    items = jnp.searchsorted(jnp.cumsum(sizes), jnp.arange(rows * top), side="right").astype(jnp.int32)
    grid = items.reshape(top, rows).T
    grid = grid[jax.random.permutation(jax.random.fold_in(own, 1), rows)]
    turn = jax.random.randint(jax.random.fold_in(own, 2), (rows, 1), 0, top)
    return jnp.take_along_axis(grid, (jnp.arange(top)[None, :] + turn) % top, axis=1)


def portions_of(amount, total, reach, slope, full):
    loads = [(1 << 20) // math.isqrt(rank ** slope) + 1 for rank in range(1, amount + 1)]
    largest = reach if full else min(reach, max(-(-total // amount), total * loads[0] // sum(loads)))
    least = 1 if total - largest >= amount - 1 else 0
    holding, rest = [largest] + [least] * (amount - 1), total - largest - least * (amount - 1)
    while rest > 0:
        free = [i for i in range(1, amount) if holding[i] < largest] or [i for i in range(1, amount) if holding[i] < reach]
        whole, budget = sum([loads[i] for i in free]), rest
        for i in free:
            extra = min(reach - holding[i], max(1, budget * loads[i] // whole), rest)
            holding[i] = holding[i] + extra
            rest = rest - extra
    return np.array(holding)


def centred(stream_key, dims, spread, most, shards=(), held_as=jnp.bfloat16):
    factor_of = shard_levels(stream_key, dims, shards, -0.22, 0.18) if shards else 1.0
    result = jax.random.normal(stream_key, dims, jnp.float32) * spread * factor_of
    return jnp.minimum(jnp.maximum(result, -most), most).astype(held_as)


def setup_inputs(seed: int = 0) -> dict:
    key_list = jax.random.split(jax.random.key(seed), 11)
    attn = centred(key_list[0], (TOKENS, D), 1.0, 6.0, ((0, 16), (1, 2)))
    resid = centred(key_list[1], (TOKENS, D), 1.0, 6.0, ((0, 16), (1, 2)))
    w_out = centred(key_list[2], (D, D), D ** -0.5, 0.15625, ((0, 2), (1, 16)))
    gain_mix = jnp.clip(1.0 + 0.18 * jax.random.normal(key_list[3], (D,), jnp.float32), 0.1, 1.9)
    gain_out = jnp.clip(1.0 + 0.18 * jax.random.normal(key_list[4], (D,), jnp.float32), 0.1, 1.9)
    routes_keys = jax.random.split(jax.random.fold_in(key_list[5], 1), TOKENS // BLOCK)
    routes_turns = jax.random.permutation(jax.random.fold_in(key_list[5], 3), TOKENS // BLOCK)
    routes = jax.vmap(lambda own, number: shared_out(jax.random.fold_in(key_list[5], 2), own, number, BLOCK, EXPERTS, TOPK, MOST, 2))(routes_keys, routes_turns).reshape((TOKENS, TOPK))
    gates = jnp.clip(jnp.exp(math.log(1.0) - 2.9957323 * jax.random.uniform(key_list[6], (TOKENS, TOPK), jnp.float32) ** shard_levels(key_list[6], (TOKENS, TOPK), ((0, 16),), -0.2, 0.2)), 0.05, 1.0)
    w_gate = draw_w_gate(jax.random.fold_in(key_list[10], 71), 0)
    w_up = draw_w_up(jax.random.fold_in(key_list[10], 71), 0)
    w_down = draw_w_down(jax.random.fold_in(key_list[10], 71), 0)
    return dict(attn=attn, resid=resid, w_out=w_out, gain_mix=gain_mix, gain_out=gain_out, routes=routes, gates=gates, w_gate=w_gate, w_up=w_up, w_down=w_down)


epsilon = 1e-05

def rms_scale(values, gain):
    return values * lax.rsqrt(lax.optimization_barrier(jnp.mean(values * values, axis=1, keepdims=True)) + epsilon) * gain

def reference(attn, resid, w_out, gain_mix, gain_out, routes, gates, w_gate, w_up, w_down):
    hidden = resid.astype(jnp.float32) + jnp.dot(attn, w_out, preferred_element_type=jnp.float32)
    normed = rms_scale(hidden, gain_mix).astype(jnp.bfloat16)
    capacity = TOKENS // BLOCK * MOST

    def one_expert(total, expert):
        hit = routes == expert
        weight = lax.optimization_barrier(jnp.sum(jnp.where(hit, gates, jnp.zeros_like(gates)), axis=1))
        routed = jnp.any(hit, axis=1)
        row_index = jnp.nonzero(routed, size=capacity, fill_value=0)[0].astype(jnp.int32)
        is_live = jnp.arange(capacity) < jnp.sum(routed.astype(jnp.int32))
        gathered = normed[row_index]
        gate_pre = jnp.dot(gathered, w_gate[expert], preferred_element_type=jnp.float32)
        up_pre = jnp.dot(gathered, w_up[expert], preferred_element_type=jnp.float32)
        activated = (jax.nn.silu(gate_pre) * up_pre).astype(jnp.bfloat16)
        expert_out = jnp.dot(activated, w_down[expert], preferred_element_type=jnp.float32).astype(jnp.bfloat16)
        scale_rows = jnp.where(is_live, weight[row_index], jnp.zeros_like(weight[row_index]))
        contrib = expert_out.astype(jnp.float32) * scale_rows[:, None]
        return (total.at[row_index].add(contrib), None)
    total, _ = lax.scan(one_expert, jnp.zeros(hidden.shape, jnp.float32), jnp.arange(EXPERTS, dtype=jnp.int32))
    combined = hidden + total
    return rms_scale(combined, gain_out).astype(jnp.bfloat16)
```

```python
import functools

import jax
import jax.numpy as jnp
from jax import lax
from jax.experimental import pallas as pl
from jax.experimental.pallas import tpu as pltpu
from jax.sharding import PartitionSpec as P

EXPERTS = 40
EPSILON = 1e-05
CHUNKS = 2
MESH = pl.DeviceIdType.MESH


def chip_at(place, chips):
    far = place // (chips // 2)
    return (1 - far) * (2 * place) + far * (2 * (chips - 1 - place) + 1)


def place_of(chip, chips):
    odd = chip % 2
    return (1 - odd) * (chip // 2) + odd * (chips - 1 - chip // 2)


def layer_kernel(
    tp_count, chips, rows, width, local, cap, split_out,
    parts_ref, own_ref, table_ref, gain_mix_ref, gain_out_ref, gate_hbm, up_hbm, down_hbm,
    out_ref,
    tokens, sums, away, from_pair, from_prev, from_next, hidden, part_in, w_gate, w_up, w_down,
    picked, pick_mats, scaled, finished,
    weight_sem, part_send, part_recv, right_send, right_recv, left_send, left_recv,
    pair_send, pair_recv, down_send, down_recv, back_send, back_recv, cross_send, cross_recv,
    out_send, out_recv,
):
    half = chips // 2
    step_rows = rows // CHUNKS
    mid = width // 2
    ep = lax.axis_index("ep")
    tp = lax.axis_index("tp")
    core = ep % 2
    place = place_of(ep // 2, chips)
    after = chip_at((place + 1) % chips, chips) * 2 + core
    before = chip_at((place + chips - 1) % chips, chips) * 2 + core
    pair = ep + 1 - 2 * core

    barrier = pltpu.get_barrier_semaphore()
    for other in (after, before, pair):
        pl.semaphore_signal(barrier, inc=1, device_id={"ep": other}, device_id_type=MESH)
    for k in range(1, tp_count):
        pl.semaphore_signal(barrier, inc=1, device_id={"tp": (tp + k) % tp_count}, device_id_type=MESH)
    pl.semaphore_wait(barrier, 3 + tp_count - 1)

    loads = [
        pltpu.make_async_copy(src, dst, weight_sem.at[i])
        for i, (src, dst) in enumerate(((gate_hbm, w_gate), (up_hbm, w_up), (down_hbm, w_down)))
    ]

    def to_ep(src, dst, send, recv, other):
        return pltpu.make_async_remote_copy(
            src_ref=src, dst_ref=dst, send_sem=send, recv_sem=recv,
            device_id={"ep": other}, device_id_type=MESH)

    def to_tp(src, dst, send, recv, k):
        return pltpu.make_async_remote_copy(
            src_ref=src, dst_ref=dst, send_sem=send, recv_sem=recv,
            device_id={"tp": (tp + k) % tp_count}, device_id_type=MESH)

    def band(c):
        return pl.ds(c * step_rows, step_rows)

    def part_copy(k, c):
        return to_tp(parts_ref.at[(tp + k) % tp_count, band(c)], part_in.at[k - 1, band(c)],
                     part_send.at[k - 1, c], part_recv.at[k - 1, c], k)

    for c in range(CHUNKS):
        for k in range(1, tp_count):
            part_copy(k, c).start()
    for load in loads:
        load.start()

    def right_copy(t, c):
        return to_ep(tokens.at[t - 1, 0, band(c)], tokens.at[t, 0, band(c)],
                     right_send.at[t - 1, c], right_recv.at[t - 1, c], after)

    def left_copy(t, c):
        return to_ep(tokens.at[(chips - t + 1) % chips, 0, band(c)], tokens.at[chips - t, 0, band(c)],
                     left_send.at[t - 1, c], left_recv.at[t - 1, c], before)

    def right_last(c):
        return to_ep(tokens.at[half - 1, 0, band(c), pl.ds(0, mid)], tokens.at[half, 0, band(c), pl.ds(0, mid)],
                     right_send.at[half - 1, c], right_recv.at[half - 1, c], after)

    def left_last(c):
        return to_ep(tokens.at[half + 1, 0, band(c), pl.ds(mid, mid)], tokens.at[half, 0, band(c), pl.ds(mid, mid)],
                     left_send.at[half - 1, c], left_recv.at[half - 1, c], before)

    def pair_copy(s, c):
        return to_ep(tokens.at[s, 0, band(c)], tokens.at[s, 1, band(c)],
                     pair_send.at[s, c], pair_recv.at[s, c], pair)

    small = min(32, step_rows)

    def norm_rows(at, gain_ref, add):
        value = add(at)
        scale = lax.rsqrt(jnp.mean(value * value, axis=1, keepdims=True) + EPSILON)
        return value, (value * scale * gain_ref[...]).astype(jnp.bfloat16)

    for c in range(CHUNKS):
        for k in range(1, tp_count):
            part_copy(k, c).wait_recv()

        def mix(i, carry):
            at = pl.ds(pl.multiple_of(c * step_rows + i * small, small), small)

            def add(at):
                value = own_ref[at, :]
                for k in range(1, tp_count):
                    value = value + part_in[k - 1, at, :].astype(jnp.float32)
                return value

            value, normed = norm_rows(at, gain_mix_ref, add)
            hidden[at, :] = value
            tokens[0, 0, at, :] = normed
            return carry

        lax.fori_loop(0, step_rows // small, mix, 0)
        right_copy(1, c).start()
        left_copy(1, c).start()
        pair_copy(0, c).start()
    for load in loads:
        load.wait()

    def experts(blocks):
        where = []
        for slot, which, _ in blocks:
            chip = chip_at((place + chips - slot) % chips, chips)
            where.append(chip * 2 + (core + which - 2 * core * which))
        count = len(blocks)

        def one(f, carry):
            at = pl.ds(pl.multiple_of(f * cap, cap), cap)
            columns = []
            for b, (slot, which, _) in enumerate(blocks):
                place_row = table_ref[where[b], pl.ds(f, 1), :]
                gate_row = table_ref[where[b], pl.ds(local + f, 1), :]
                index = lax.broadcasted_iota(jnp.int32, (cap, rows), 0).astype(jnp.float32)
                hit = index == place_row
                columns.append(jnp.sum(jnp.where(hit, gate_row, 0.0), axis=1, keepdims=True))
                choose = jnp.where(hit, 1.0, 0.0).astype(jnp.bfloat16)
                pick_mats[b, at, :] = choose
                picked[pl.ds(b * cap, cap), :] = jnp.dot(
                    choose, tokens[slot, which], preferred_element_type=jnp.float32).astype(jnp.bfloat16)
            rows_in = picked[pl.ds(0, count * cap), :]
            gate = jnp.dot(rows_in, w_gate[f], preferred_element_type=jnp.float32)
            up = jnp.dot(rows_in, w_up[f], preferred_element_type=jnp.float32)
            act = (gate / (1.0 + jnp.exp(-gate)) * up).astype(jnp.bfloat16)
            result = jnp.dot(act, w_down[f], preferred_element_type=jnp.float32)
            for b in range(count):
                scaled[b, at, :] = (result[b * cap:(b + 1) * cap, :] * columns[b]).astype(jnp.bfloat16)
            return carry

        lax.fori_loop(0, local, one, 0)
        for b, (_, _, target) in enumerate(blocks):
            target[...] = lax.dot_general(
                pick_mats[b], scaled[b], (((0,), (0,)), ((), ())),
                preferred_element_type=jnp.float32).astype(jnp.bfloat16)

    def cross_copy(s, buffer):
        return to_ep(away.at[buffer], from_pair.at[s], cross_send.at[s], cross_recv.at[s], pair)

    def step(t, carry):
        for c in range(CHUNKS):
            right_copy(t, c).wait_recv()

            @pl.when(t < half - 1)
            def _():
                right_copy(t + 1, c).start()

            @pl.when(t == half - 1)
            def _():
                right_last(c).start()

            pair_copy(t, c).start()
            left_copy(t, c).wait_recv()

            @pl.when(t < half - 1)
            def _():
                left_copy(t + 1, c).start()

            @pl.when(t == half - 1)
            def _():
                left_last(c).start()

            pair_copy(chips - t, c).start()
        for c in range(CHUNKS):
            pair_copy(t, c).wait_recv()
            pair_copy(chips - t, c).wait_recv()
        turn = t % 2

        @pl.when(t > 2)
        def _():
            cross_copy(t - 2, 2 * turn).wait_send()
            cross_copy(chips - t + 2, 2 * turn + 1).wait_send()

        experts([
            (t, 0, sums.at[t]), (t, 1, away.at[2 * turn]),
            (chips - t, 0, sums.at[chips - t]), (chips - t, 1, away.at[2 * turn + 1]),
        ])
        cross_copy(t, 2 * turn).start()
        cross_copy(chips - t, 2 * turn + 1).start()
        return carry

    lax.fori_loop(1, half, step, 0)

    for c in range(CHUNKS):
        right_last(c).wait_recv()
        left_last(c).wait_recv()
        pair_copy(half, c).start()
    for c in range(CHUNKS):
        pair_copy(half, c).wait_recv()
    turn_a, turn_b = half % 2, (half - 1) % 2
    if half > 2:
        cross_copy(half - 2, 2 * turn_a).wait_send()
        cross_copy(chips - half + 2, 2 * turn_a + 1).wait_send()
    experts([(half, 0, sums.at[half]), (half, 1, away.at[2 * turn_a])])
    cross_copy(half, 2 * turn_a).start()

    def add_rows(s, at, extra, columns=slice(None)):
        def body(i, carry):
            here = pl.ds(pl.multiple_of(at + i * small, small), small)
            value = sums[s, here, columns].astype(jnp.float32) + from_pair[s, here, columns].astype(jnp.float32)
            if extra is not None:
                value = value + extra[here, columns].astype(jnp.float32)
            sums[s, here, columns] = value.astype(jnp.bfloat16)
            return carry

        lax.fori_loop(0, step_rows // small, body, 0)

    def down_first(c):
        return to_ep(sums.at[half, band(c), pl.ds(0, mid)], from_prev.at[half - 1, band(c), pl.ds(0, mid)],
                     down_send.at[half - 1, c], down_recv.at[half - 1, c], after)

    def back_first(c):
        return to_ep(sums.at[half, band(c), pl.ds(mid, mid)], from_next.at[half - 1, band(c), pl.ds(mid, mid)],
                     back_send.at[half - 1, c], back_recv.at[half - 1, c], before)

    def down_copy(t, c):
        return to_ep(sums.at[chips - t, band(c)], from_prev.at[t - 1, band(c)],
                     down_send.at[t - 1, c], down_recv.at[t - 1, c], after)

    def back_copy(t, c):
        return to_ep(sums.at[t, band(c)], from_next.at[t - 1, band(c)],
                     back_send.at[t - 1, c], back_recv.at[t - 1, c], before)

    cross_copy(half, 2 * turn_a).wait_recv()
    for c in range(CHUNKS):
        add_rows(half, c * step_rows, None)
        down_first(c).start()
        back_first(c).start()

    for c in range(CHUNKS):
        pair_copy(0, c).wait_recv()
    cross_copy(half - 1, 2 * turn_b).wait_send()
    cross_copy(chips - half + 1, 2 * turn_b + 1).wait_send()
    experts([(0, 0, sums.at[0]), (0, 1, away.at[2 * turn_b])])
    cross_copy(0, 2 * turn_b).start()

    last = half - 1
    cross_copy(last, 0).wait_recv()
    cross_copy(chips - last, 0).wait_recv()
    for c in range(CHUNKS):
        down_first(c).wait_recv()
        add_rows(chips - last, c * step_rows, from_prev.at[last], pl.ds(0, mid))
        add_rows(chips - last, c * step_rows, None, pl.ds(mid, mid))
        down_copy(last, c).start()
        back_first(c).wait_recv()
        add_rows(last, c * step_rows, None, pl.ds(0, mid))
        add_rows(last, c * step_rows, from_next.at[last], pl.ds(mid, mid))
        back_copy(last, c).start()

    def sum_step(i, carry):
        t = half - 2 - i
        cross_copy(t, 0).wait_recv()
        cross_copy(chips - t, 0).wait_recv()
        for c in range(CHUNKS):
            down_copy(t + 1, c).wait_recv()
            add_rows(chips - t, c * step_rows, from_prev.at[t])
            down_copy(t, c).start()
            back_copy(t + 1, c).wait_recv()
            add_rows(t, c * step_rows, from_next.at[t])
            back_copy(t, c).start()
        return carry

    lax.fori_loop(0, half - 2, sum_step, 0)
    cross_copy(0, 0).wait_recv()

    part_width = width // tp_count

    def out_copy(k, c):
        at = pl.ds(tp * rows + c * step_rows, step_rows)
        return to_tp(finished.at[(tp + k) % tp_count, band(c)], out_ref.at[at],
                     out_send.at[k - 1, c], out_recv.at[k - 1, c], k)

    for c in range(CHUNKS):
        down_copy(1, c).wait_recv()
        back_copy(1, c).wait_recv()

        def close(i, carry):
            at = pl.ds(pl.multiple_of(c * step_rows + i * small, small), small)

            def add(at):
                value = hidden[at, :]
                for part in (sums.at[0], from_pair.at[0], from_prev.at[0], from_next.at[0]):
                    value = value + part[at, :].astype(jnp.float32)
                return value

            _, done = norm_rows(at, gain_out_ref, add)
            if split_out:
                for r in range(tp_count):
                    finished[r, at, :] = done[:, r * part_width:(r + 1) * part_width]
            else:
                out_ref[at, :] = done
            return carry

        lax.fori_loop(0, step_rows // small, close, 0)
        if split_out:
            for k in range(1, tp_count):
                out_copy(k, c).start()

            def keep(i, carry):
                at = pl.multiple_of(c * step_rows + i * small, small)
                out_ref[pl.ds(tp * rows + at, small), :] = finished[tp, pl.ds(at, small), :]
                return carry

            lax.fori_loop(0, step_rows // small, keep, 0)

    for c in range(CHUNKS):
        for k in range(1, tp_count):
            part_copy(k, c).wait_send()
            if split_out:
                out_copy(k, c).wait_send()
                out_copy(k, c).wait_recv()
        right_last(c).wait_send()
        left_last(c).wait_send()
        down_first(c).wait_send()
        back_first(c).wait_send()

    def drain(i, carry):
        t = i + 1
        for c in range(CHUNKS):
            right_copy(t, c).wait_send()
            left_copy(t, c).wait_send()
            down_copy(t, c).wait_send()
            back_copy(t, c).wait_send()
        return carry

    lax.fori_loop(0, half - 1, drain, 0)

    def drain_pair(s, carry):
        for c in range(CHUNKS):
            pair_copy(s, c).wait_send()
        return carry

    lax.fori_loop(0, chips, drain_pair, 0)
    cross_copy(half, 2 * turn_a).wait_send()
    cross_copy(0, 2 * turn_b).wait_send()


def per_device(attn, resid, w_out, gain_mix, gain_out, routes, gates, w_gate, w_up, w_down):
    tp_count = lax.axis_size("tp")
    tp_rank = lax.axis_index("tp")
    ep_count = lax.axis_size("ep")
    ep_rank = lax.axis_index("ep")
    tok_dev, width_part = attn.shape
    width = width_part * tp_count
    rows = tok_dev // tp_count
    topk = routes.shape[1]
    local, _, hidden_units = w_gate.shape
    cap = rows * topk // 32
    chips = ep_count // 2
    half = chips // 2
    split_out = width_part % 128 == 0

    my_routes = lax.dynamic_slice_in_dim(routes, tp_rank * rows, rows, 0)
    my_gates = lax.dynamic_slice_in_dim(gates, tp_rank * rows, rows, 0)
    both = jnp.concatenate([my_routes.T.astype(jnp.float32), my_gates.T], axis=0)
    both = lax.all_gather(both, "ep", axis=0)
    slot = ep_rank * local + jnp.arange(local, dtype=jnp.int32)
    expert = jnp.where(slot < EXPERTS, slot, -1).astype(jnp.float32)
    named = both[:, None, :topk, :] == expert[None, :, None, None]
    hit = jnp.any(named, axis=2)
    weight = jnp.sum(jnp.where(named, both[:, None, topk:, :], 0.0), axis=2)
    earlier = jnp.triu(jnp.ones((rows, rows), jnp.bfloat16), 1)
    rank = jnp.einsum("bfi,ij->bfj", hit.astype(jnp.bfloat16), earlier, preferred_element_type=jnp.float32)
    table = jnp.concatenate([jnp.where(hit, rank, -1.0), weight], axis=1)
    table = jnp.pad(table, ((0, 0), (0, -(2 * local) % 8), (0, 0)))

    columns = lax.all_gather(w_out, "ep", axis=1, tiled=True)
    part = jnp.dot(attn, columns, preferred_element_type=jnp.float32)
    spread = lax.dynamic_update_slice(jnp.zeros((tok_dev, width), resid.dtype), resid, (0, tp_rank * width_part))
    part = part + spread.astype(jnp.float32)
    own = lax.dynamic_slice_in_dim(part, tp_rank * rows, rows, 0)
    parts = part.astype(jnp.bfloat16).reshape(tp_count, rows, width)

    bf16, f32 = jnp.bfloat16, jnp.float32
    vmem = pl.BlockSpec(memory_space=pltpu.VMEM)
    anywhere = pl.BlockSpec(memory_space=pl.ANY)
    dma = pltpu.SemaphoreType.DMA
    others = tp_count - 1
    out_shape = (tok_dev, width_part) if split_out else (rows, width)
    result = pl.pallas_call(
        functools.partial(layer_kernel, tp_count, chips, rows, width, local, cap, split_out),
        out_shape=jax.ShapeDtypeStruct(out_shape, bf16),
        in_specs=[vmem] * 5 + [anywhere] * 3,
        out_specs=vmem,
        scratch_shapes=[
            pltpu.VMEM((chips, 2, rows, width), bf16),
            pltpu.VMEM((chips, rows, width), bf16),
            pltpu.VMEM((4, rows, width), bf16),
            pltpu.VMEM((chips, rows, width), bf16),
            pltpu.VMEM((half, rows, width), bf16),
            pltpu.VMEM((half, rows, width), bf16),
            pltpu.VMEM((rows, width), f32),
            pltpu.VMEM((others, rows, width), bf16),
            pltpu.VMEM(w_gate.shape, bf16),
            pltpu.VMEM(w_up.shape, bf16),
            pltpu.VMEM(w_down.shape, bf16),
            pltpu.VMEM((4 * cap, width), bf16),
            pltpu.VMEM((4, local * cap, rows), bf16),
            pltpu.VMEM((4, local * cap, width), bf16),
            pltpu.VMEM((tp_count, rows, width_part), bf16),
            dma((3,)),
            dma((others, CHUNKS)), dma((others, CHUNKS)),
            dma((half, CHUNKS)), dma((half, CHUNKS)),
            dma((half, CHUNKS)), dma((half, CHUNKS)),
            dma((chips, CHUNKS)), dma((chips, CHUNKS)),
            dma((half, CHUNKS)), dma((half, CHUNKS)),
            dma((half, CHUNKS)), dma((half, CHUNKS)),
            dma((chips,)), dma((chips,)),
            dma((others, CHUNKS)), dma((others, CHUNKS)),
        ],
        compiler_params=pltpu.CompilerParams(
            collective_id=0, has_side_effects=True, vmem_limit_bytes=63 * 1024 * 1024),
    )(parts, own, table, gain_mix.reshape(1, width), gain_out.reshape(1, width), w_gate, w_up, w_down)
    if split_out:
        return result
    return lax.all_to_all(result, "tp", split_axis=1, concat_axis=0, tiled=True)


def solution(mesh):
    return jax.shard_map(
        per_device,
        mesh=mesh,
        in_specs=(
            P("ep", "tp"),
            P("ep", "tp"),
            P("tp", "ep"),
            P(),
            P(),
            P("ep", None),
            P("ep", None),
            P("ep", None, None),
            P("ep", None, None),
            P("ep", None, None),
        ),
        out_specs=P("ep", "tp"),
        check_vma=False,
    )
```

```python
import functools

import jax
import jax.numpy as jnp
from jax import lax
from jax.experimental import pallas as pl
from jax.experimental.pallas import tpu as pltpu
from jax.sharding import PartitionSpec as P

EXPERTS = 40
EPSILON = 1e-05
CHUNKS = 4
MESH = pl.DeviceIdType.MESH


def chip_at(place, chips):
    far = place // (chips // 2)
    return (1 - far) * (2 * place) + far * (2 * (chips - 1 - place) + 1)


def place_of(chip, chips):
    odd = chip % 2
    return (1 - odd) * (chip // 2) + odd * (chips - 1 - chip // 2)


def layer_kernel(
    tp_count, chips, rows, width, local, cap, topk, inside,
    *refs,
):
    if inside:
        attn_ref, resid_ref, w_part, *refs = refs
    else:
        parts_ref, own_ref, *refs = refs
    split_out = inside
    (routed_ref, gains, gate_hbm, up_hbm, down_hbm, out_ref, *refs) = refs
    if inside:
        parts_ref, w_all, w_pair_send, w_pair_recv, w_send, w_recv, *refs = refs
    (
    tokens, sums, away, from_pair, from_prev, from_next, hidden, part_in, w_gate, w_up, w_down,
    picked, pick_mats, scaled, finished,
    weight_sem, part_send, part_recv, right_send, right_recv, left_send, left_recv,
    pair_send, pair_recv, down_send, down_recv, back_send, back_recv, cross_send, cross_recv,
    out_send, out_recv,
    routed, places, shares, r_pair_send, r_pair_recv, r_send, r_recv,
    ) = refs
    half = chips // 2
    step_rows = rows // CHUNKS
    mid = width // 2
    ep = lax.axis_index("ep")
    tp = lax.axis_index("tp")
    core = ep % 2
    place = place_of(ep // 2, chips)
    after = chip_at((place + 1) % chips, chips) * 2 + core
    before = chip_at((place + chips - 1) % chips, chips) * 2 + core
    pair = ep + 1 - 2 * core

    barrier = pltpu.get_barrier_semaphore()
    for other in (after, before, pair):
        pl.semaphore_signal(barrier, inc=1, device_id={"ep": other}, device_id_type=MESH)
    for k in range(1, tp_count):
        pl.semaphore_signal(barrier, inc=1, device_id={"tp": (tp + k) % tp_count}, device_id_type=MESH)
    pl.semaphore_wait(barrier, 3 + tp_count - 1)

    loads = [
        pltpu.make_async_copy(src, dst, weight_sem.at[i])
        for i, (src, dst) in enumerate(((gate_hbm, w_gate), (up_hbm, w_up), (down_hbm, w_down)))
    ]

    def to_ep(src, dst, send, recv, other):
        return pltpu.make_async_remote_copy(
            src_ref=src, dst_ref=dst, send_sem=send, recv_sem=recv,
            device_id={"ep": other}, device_id_type=MESH)

    def to_tp(src, dst, send, recv, k):
        return pltpu.make_async_remote_copy(
            src_ref=src, dst_ref=dst, send_sem=send, recv_sem=recv,
            device_id={"tp": (tp + k) % tp_count}, device_id_type=MESH)

    def band(c):
        return pl.ds(c * step_rows, step_rows)

    def part_copy(k, c):
        return to_tp(parts_ref.at[k - 1 if inside else (tp + k) % tp_count, band(c)], part_in.at[k - 1, band(c)],
                     part_send.at[k - 1, c], part_recv.at[k - 1, c], k)

    def device_at(back, which=0):
        return chip_at((place + chips + back) % chips, chips) * 2 + (core + which - 2 * core * which)

    def routes_ring(t, way):
        held = routed.at[device_at(-way * (t - 1))]
        return to_ep(held, routed.at[device_at(-way * (t - 1))],
                     r_send.at[(1 - way) // 2, t - 1], r_recv.at[(1 - way) // 2, t - 1],
                     after if way == 1 else before)

    def routes_got(t, way):
        held = routed.at[device_at(-way * t)]
        return to_ep(held, held, r_send.at[(1 - way) // 2, t - 1], r_recv.at[(1 - way) // 2, t - 1],
                     after if way == 1 else before)

    def routes_pair(s, which):
        held = routed.at[device_at(-s, which)]
        return to_ep(held, held, r_pair_send.at[s], r_pair_recv.at[s], pair)

    if inside:
        columns = w_part.shape[0]

        def w_rows(device, t, way):
            if t < half:
                return w_all.at[pl.ds(device * columns, columns)]
            part = columns // 2
            return w_all.at[pl.ds(device * columns + (0 if way == 1 else part), part)]

        def w_ring(t, way, got=0):
            held = w_rows(device_at(-way * (t - 1 + got)), t, way)
            return to_ep(held, held, w_send.at[(1 - way) // 2, t - 1], w_recv.at[(1 - way) // 2, t - 1],
                         after if way == 1 else before)

        def w_pair(s, which):
            held = w_all.at[pl.ds(device_at(-s, which) * columns, columns)]
            return to_ep(held, held, w_pair_send.at[s], w_pair_recv.at[s], pair)

        w_all[pl.ds(ep * columns, columns), :] = w_part[...]
    routed[ep] = routed_ref[...]
    for t in range(1, half + 1):
        for way in (1, -1):
            if t > 1 and inside:
                w_ring(t - 1, way, 1).wait_recv()
            if inside:
                w_ring(t, way).start()
        if inside:
            if t == 1:
                w_pair(0, 0).start()
            else:
                w_pair(t - 1, 0).start()
                w_pair(chips - t + 1, 0).start()
        for way in (1, -1):
            if t > 1:
                routes_got(t - 1, way).wait_recv()
            if t < half or way == 1:
                routes_ring(t, way).start()
        if t == 1:
            routes_pair(0, 0).start()
        else:
            routes_pair(t - 1, 0).start()
            routes_pair(chips - t + 1, 0).start()
    if inside:
        w_ring(half, 1, 1).wait_recv()
        w_ring(half, -1, 1).wait_recv()
        w_pair(half, 0).start()
    routes_got(half, 1).wait_recv()
    routes_pair(half, 0).start()
    if inside:
        for s in range(chips):
            w_pair(s, 1).wait_recv()

        part_width = width // tp_count
        mine = pl.ds(pl.multiple_of(tp * part_width, 128), part_width)

        def project(k, c):
            first = ((tp + k) % tp_count) * rows + c * step_rows
            from_rows = pl.ds(pl.multiple_of(first, step_rows), step_rows)
            hidden[band(c), :] = lax.dot_general(
                attn_ref[from_rows, :], w_all[...], (((1,), (1,)), ((), ())),
                preferred_element_type=jnp.float32)
            hidden[band(c), mine] = hidden[band(c), mine] + resid_ref[from_rows, :].astype(jnp.float32)

        for k in range(1, tp_count):
            for c in range(CHUNKS):
                project(k, c)
                parts_ref[k - 1, band(c), :] = hidden[band(c), :].astype(jnp.bfloat16)
                part_copy(k, c).start()
        for c in range(CHUNKS):
            project(0, c)
    else:
        for c in range(CHUNKS):
            for k in range(1, tp_count):
                part_copy(k, c).start()
    for load in loads:
        load.start()
    for s in range(chips):
        routes_pair(s, 1).wait_recv()

    earlier = jnp.where(
        lax.broadcasted_iota(jnp.int32, (rows, rows), 0) < lax.broadcasted_iota(jnp.int32, (rows, rows), 1),
        1.0, 0.0).astype(jnp.bfloat16)

    def lay_out(block, carry):
        names = routed[block, pl.ds(0, topk), :]
        weights = routed[block, pl.ds(topk, topk), :]
        hits = []
        for f in range(local):
            slot = ep * local + f
            expert = jnp.where(slot < EXPERTS, slot, -1).astype(jnp.float32)
            named = names == expert
            hits.append(jnp.max(jnp.where(named, 1.0, 0.0), axis=0, keepdims=True))
            shares[block, pl.ds(f, 1), :] = jnp.sum(jnp.where(named, weights, 0.0), axis=0, keepdims=True)
        hits = hits + [jnp.zeros((1, rows), jnp.float32)] * (8 - local)
        hits = jnp.concatenate(hits, axis=0)
        rank = jnp.dot(hits.astype(jnp.bfloat16), earlier, preferred_element_type=jnp.float32)
        places[block] = jnp.where(hits > 0.5, rank, -1.0)
        return carry

    lax.fori_loop(0, 2 * chips, lay_out, 0)

    def right_copy(t, c):
        return to_ep(tokens.at[t - 1, 0, band(c)], tokens.at[t, 0, band(c)],
                     right_send.at[t - 1, c], right_recv.at[t - 1, c], after)

    def left_copy(t, c):
        return to_ep(tokens.at[(chips - t + 1) % chips, 0, band(c)], tokens.at[chips - t, 0, band(c)],
                     left_send.at[t - 1, c], left_recv.at[t - 1, c], before)

    def right_last(c):
        return to_ep(tokens.at[half - 1, 0, band(c), pl.ds(0, mid)], tokens.at[half, 0, band(c), pl.ds(0, mid)],
                     right_send.at[half - 1, c], right_recv.at[half - 1, c], after)

    def left_last(c):
        return to_ep(tokens.at[half + 1, 0, band(c), pl.ds(mid, mid)], tokens.at[half, 0, band(c), pl.ds(mid, mid)],
                     left_send.at[half - 1, c], left_recv.at[half - 1, c], before)

    def pair_copy(s, c):
        return to_ep(tokens.at[s, 0, band(c)], tokens.at[s, 1, band(c)],
                     pair_send.at[s, c], pair_recv.at[s, c], pair)

    small = min(32, step_rows)

    def norm_rows(at, which, add):
        value = add(at)
        scale = lax.rsqrt(jnp.mean(value * value, axis=1, keepdims=True) + EPSILON)
        return value, (value * scale * gains[pl.ds(which, 1), :]).astype(jnp.bfloat16)

    for c in range(CHUNKS):
        for k in range(1, tp_count):
            part_copy(k, c).wait_recv()

        def mix(i, carry):
            at = pl.ds(pl.multiple_of(c * step_rows + i * small, small), small)

            def add(at):
                value = (hidden if inside else own_ref)[at, :]
                for k in range(1, tp_count):
                    value = value + part_in[k - 1, at, :].astype(jnp.float32)
                return value

            value, normed = norm_rows(at, 0, add)
            hidden[at, :] = value
            tokens[0, 0, at, :] = normed
            return carry

        lax.fori_loop(0, step_rows // small, mix, 0)
        right_copy(1, c).start()
        left_copy(1, c).start()
        pair_copy(0, c).start()
    for load in loads:
        load.wait()

    def experts(blocks):
        where = []
        for slot, which, _ in blocks:
            chip = chip_at((place + chips - slot) % chips, chips)
            where.append(chip * 2 + (core + which - 2 * core * which))
        count = len(blocks)

        def one(f, carry):
            at = pl.ds(pl.multiple_of(f * cap, cap), cap)
            columns = []
            for b, (slot, which, _) in enumerate(blocks):
                place_row = places[where[b], pl.ds(f, 1), :]
                gate_row = shares[where[b], pl.ds(f, 1), :]
                index = lax.broadcasted_iota(jnp.int32, (cap, rows), 0).astype(jnp.float32)
                hit = index == place_row
                columns.append(jnp.sum(jnp.where(hit, gate_row, 0.0), axis=1, keepdims=True))
                choose = jnp.where(hit, 1.0, 0.0).astype(jnp.bfloat16)
                pick_mats[b, at, :] = choose
                picked[pl.ds(b * cap, cap), :] = jnp.dot(
                    choose, tokens[slot, which], preferred_element_type=jnp.float32).astype(jnp.bfloat16)
            rows_in = picked[pl.ds(0, count * cap), :]
            gate = jnp.dot(rows_in, w_gate[f], preferred_element_type=jnp.float32)
            up = jnp.dot(rows_in, w_up[f], preferred_element_type=jnp.float32)
            act = (gate / (1.0 + jnp.exp(-gate)) * up).astype(jnp.bfloat16)
            result = jnp.dot(act, w_down[f], preferred_element_type=jnp.float32)
            for b in range(count):
                scaled[b, at, :] = (result[b * cap:(b + 1) * cap, :] * columns[b]).astype(jnp.bfloat16)
            return carry

        lax.fori_loop(0, local, one, 0)
        for b, (_, _, target) in enumerate(blocks):
            target[...] = lax.dot_general(
                pick_mats[b], scaled[b], (((0,), (0,)), ((), ())),
                preferred_element_type=jnp.float32).astype(jnp.bfloat16)

    def cross_copy(s, buffer):
        return to_ep(away.at[buffer], from_pair.at[s], cross_send.at[s], cross_recv.at[s], pair)

    def step(t, carry):
        for c in range(CHUNKS):
            right_copy(t, c).wait_recv()

            @pl.when(t < half - 1)
            def _():
                right_copy(t + 1, c).start()

            @pl.when(t == half - 1)
            def _():
                right_last(c).start()

            pair_copy(t, c).start()
            left_copy(t, c).wait_recv()

            @pl.when(t < half - 1)
            def _():
                left_copy(t + 1, c).start()

            @pl.when(t == half - 1)
            def _():
                left_last(c).start()

            pair_copy(chips - t, c).start()
        for c in range(CHUNKS):
            pair_copy(t, c).wait_recv()
            pair_copy(chips - t, c).wait_recv()
        turn = t % 2

        @pl.when(t > 2)
        def _():
            cross_copy(t - 2, 2 * turn).wait_send()
            cross_copy(chips - t + 2, 2 * turn + 1).wait_send()

        experts([
            (t, 0, sums.at[t]), (t, 1, away.at[2 * turn]),
            (chips - t, 0, sums.at[chips - t]), (chips - t, 1, away.at[2 * turn + 1]),
        ])
        cross_copy(t, 2 * turn).start()
        cross_copy(chips - t, 2 * turn + 1).start()
        return carry

    lax.fori_loop(1, half, step, 0)

    for c in range(CHUNKS):
        right_last(c).wait_recv()
        left_last(c).wait_recv()
        pair_copy(half, c).start()
    for c in range(CHUNKS):
        pair_copy(half, c).wait_recv()
    turn_a, turn_b = half % 2, (half - 1) % 2
    if half > 2:
        cross_copy(half - 2, 2 * turn_a).wait_send()
        cross_copy(chips - half + 2, 2 * turn_a + 1).wait_send()
    experts([(half, 0, sums.at[half]), (half, 1, away.at[2 * turn_a])])
    cross_copy(half, 2 * turn_a).start()

    def add_rows(s, at, extra, columns=slice(None)):
        def body(i, carry):
            here = pl.ds(pl.multiple_of(at + i * small, small), small)
            value = sums[s, here, columns].astype(jnp.float32) + from_pair[s, here, columns].astype(jnp.float32)
            if extra is not None:
                value = value + extra[here, columns].astype(jnp.float32)
            sums[s, here, columns] = value.astype(jnp.bfloat16)
            return carry

        lax.fori_loop(0, step_rows // small, body, 0)

    def down_first(c):
        return to_ep(sums.at[half, band(c), pl.ds(0, mid)], from_prev.at[half - 1, band(c), pl.ds(0, mid)],
                     down_send.at[half - 1, c], down_recv.at[half - 1, c], after)

    def back_first(c):
        return to_ep(sums.at[half, band(c), pl.ds(mid, mid)], from_next.at[half - 1, band(c), pl.ds(mid, mid)],
                     back_send.at[half - 1, c], back_recv.at[half - 1, c], before)

    def down_copy(t, c):
        return to_ep(sums.at[chips - t, band(c)], from_prev.at[t - 1, band(c)],
                     down_send.at[t - 1, c], down_recv.at[t - 1, c], after)

    def back_copy(t, c):
        return to_ep(sums.at[t, band(c)], from_next.at[t - 1, band(c)],
                     back_send.at[t - 1, c], back_recv.at[t - 1, c], before)

    cross_copy(half, 2 * turn_a).wait_recv()
    for c in range(CHUNKS):
        add_rows(half, c * step_rows, None)
        down_first(c).start()
        back_first(c).start()

    for c in range(CHUNKS):
        pair_copy(0, c).wait_recv()
    cross_copy(half - 1, 2 * turn_b).wait_send()
    cross_copy(chips - half + 1, 2 * turn_b + 1).wait_send()
    experts([(0, 0, sums.at[0]), (0, 1, away.at[2 * turn_b])])
    cross_copy(0, 2 * turn_b).start()

    last = half - 1
    cross_copy(last, 0).wait_recv()
    cross_copy(chips - last, 0).wait_recv()
    for c in range(CHUNKS):
        down_first(c).wait_recv()
        add_rows(chips - last, c * step_rows, from_prev.at[last], pl.ds(0, mid))
        add_rows(chips - last, c * step_rows, None, pl.ds(mid, mid))
        down_copy(last, c).start()
        back_first(c).wait_recv()
        add_rows(last, c * step_rows, None, pl.ds(0, mid))
        add_rows(last, c * step_rows, from_next.at[last], pl.ds(mid, mid))
        back_copy(last, c).start()

    def sum_step(i, carry):
        t = half - 2 - i
        cross_copy(t, 0).wait_recv()
        cross_copy(chips - t, 0).wait_recv()
        for c in range(CHUNKS):
            down_copy(t + 1, c).wait_recv()
            add_rows(chips - t, c * step_rows, from_prev.at[t])
            down_copy(t, c).start()
            back_copy(t + 1, c).wait_recv()
            add_rows(t, c * step_rows, from_next.at[t])
            back_copy(t, c).start()
        return carry

    lax.fori_loop(0, half - 2, sum_step, 0)
    cross_copy(0, 0).wait_recv()

    part_width = width // tp_count

    def out_copy(k, c):
        at = pl.ds(tp * rows + c * step_rows, step_rows)
        return to_tp(finished.at[(tp + k) % tp_count, band(c)], out_ref.at[at],
                     out_send.at[k - 1, c], out_recv.at[k - 1, c], k)

    for c in range(CHUNKS):
        down_copy(1, c).wait_recv()
        back_copy(1, c).wait_recv()

        def close(i, carry):
            at = pl.ds(pl.multiple_of(c * step_rows + i * small, small), small)

            def add(at):
                value = hidden[at, :]
                for part in (sums.at[0], from_pair.at[0], from_prev.at[0], from_next.at[0]):
                    value = value + part[at, :].astype(jnp.float32)
                return value

            _, done = norm_rows(at, 1, add)
            if split_out:
                for r in range(tp_count):
                    finished[r, at, :] = done[:, r * part_width:(r + 1) * part_width]
            else:
                out_ref[at, :] = done
            return carry

        lax.fori_loop(0, step_rows // small, close, 0)
        if split_out:
            for k in range(1, tp_count):
                out_copy(k, c).start()

            def keep(i, carry):
                at = pl.multiple_of(c * step_rows + i * small, small)
                out_ref[pl.ds(tp * rows + at, small), :] = finished[tp, pl.ds(at, small), :]
                return carry

            lax.fori_loop(0, step_rows // small, keep, 0)

    for c in range(CHUNKS):
        for k in range(1, tp_count):
            part_copy(k, c).wait_send()
            if split_out:
                out_copy(k, c).wait_send()
                out_copy(k, c).wait_recv()
        right_last(c).wait_send()
        left_last(c).wait_send()
        down_first(c).wait_send()
        back_first(c).wait_send()

    def drain(i, carry):
        t = i + 1
        for c in range(CHUNKS):
            right_copy(t, c).wait_send()
            left_copy(t, c).wait_send()
            down_copy(t, c).wait_send()
            back_copy(t, c).wait_send()
        return carry

    lax.fori_loop(0, half - 1, drain, 0)

    def drain_pair(s, carry):
        for c in range(CHUNKS):
            pair_copy(s, c).wait_send()
        return carry

    lax.fori_loop(0, chips, drain_pair, 0)
    cross_copy(half, 2 * turn_a).wait_send()
    cross_copy(0, 2 * turn_b).wait_send()
    for t in range(1, half + 1):
        for way in (1, -1):
            if t < half or way == 1:
                routes_ring(t, way).wait_send()
            if inside:
                w_ring(t, way).wait_send()
    for s in range(chips):
        routes_pair(s, 0).wait_send()
        if inside:
            w_pair(s, 0).wait_send()


def per_device(attn, resid, w_out, gain_mix, gain_out, routes, gates, w_gate, w_up, w_down):
    tp_count = lax.axis_size("tp")
    tp_rank = lax.axis_index("tp")
    ep_count = lax.axis_size("ep")
    tok_dev, width_part = attn.shape
    width = width_part * tp_count
    rows = tok_dev // tp_count
    topk = routes.shape[1]
    local, _, hidden_units = w_gate.shape
    cap = rows * topk // 32
    chips = ep_count // 2
    half = chips // 2

    my_routes = lax.dynamic_slice_in_dim(routes, tp_rank * rows, rows, 0)
    my_gates = lax.dynamic_slice_in_dim(gates, tp_rank * rows, rows, 0)
    both = jnp.concatenate([my_routes.T.astype(jnp.float32), my_gates.T], axis=0)
    gains = jnp.stack([gain_mix, gain_out])
    inside = width_part % 128 == 0 and w_out.shape[1] % 32 == 0
    if inside:
        first = (attn, resid, w_out.T)
    else:
        columns = lax.all_gather(w_out, "ep", axis=1, tiled=True)
        part = jnp.dot(attn, columns, preferred_element_type=jnp.float32)
        spread = lax.dynamic_update_slice(
            jnp.zeros((tok_dev, width), resid.dtype), resid, (0, tp_rank * width_part))
        part = part + spread.astype(jnp.float32)
        own = lax.dynamic_slice_in_dim(part, tp_rank * rows, rows, 0)
        first = (part.astype(jnp.bfloat16).reshape(tp_count, rows, width), own)

    bf16, f32 = jnp.bfloat16, jnp.float32
    vmem = pl.BlockSpec(memory_space=pltpu.VMEM)
    anywhere = pl.BlockSpec(memory_space=pl.ANY)
    dma = pltpu.SemaphoreType.DMA
    others = tp_count - 1
    out_shape = (tok_dev, width_part) if inside else (rows, width)
    result = pl.pallas_call(
        functools.partial(layer_kernel, tp_count, chips, rows, width, local, cap, topk, inside),
        out_shape=jax.ShapeDtypeStruct(out_shape, bf16),
        in_specs=[vmem] * (len(first) + 2) + [anywhere] * 3,
        out_specs=vmem,
        scratch_shapes=([
            pltpu.VMEM((others, rows, width), bf16),
            pltpu.VMEM((width, width_part), bf16),
            dma((chips,)), dma((chips,)), dma((2, half)), dma((2, half)),
        ] if inside else []) + [
            pltpu.VMEM((chips, 2, rows, width), bf16),
            pltpu.VMEM((chips, rows, width), bf16),
            pltpu.VMEM((4, rows, width), bf16),
            pltpu.VMEM((chips, rows, width), bf16),
            pltpu.VMEM((half, rows, width), bf16),
            pltpu.VMEM((half, rows, width), bf16),
            pltpu.VMEM((rows, width), f32),
            pltpu.VMEM((others, rows, width), bf16),
            pltpu.VMEM(w_gate.shape, bf16),
            pltpu.VMEM(w_up.shape, bf16),
            pltpu.VMEM(w_down.shape, bf16),
            pltpu.VMEM((4 * cap, width), bf16),
            pltpu.VMEM((4, local * cap, rows), bf16),
            pltpu.VMEM((4, local * cap, width), bf16),
            pltpu.VMEM((tp_count, rows, width_part), bf16),
            dma((3,)),
            dma((others, CHUNKS)), dma((others, CHUNKS)),
            dma((half, CHUNKS)), dma((half, CHUNKS)),
            dma((half, CHUNKS)), dma((half, CHUNKS)),
            dma((chips, CHUNKS)), dma((chips, CHUNKS)),
            dma((half, CHUNKS)), dma((half, CHUNKS)),
            dma((half, CHUNKS)), dma((half, CHUNKS)),
            dma((chips,)), dma((chips,)),
            dma((others, CHUNKS)), dma((others, CHUNKS)),
            pltpu.VMEM((ep_count, 2 * topk, rows), f32),
            pltpu.VMEM((ep_count, 8, rows), f32),
            pltpu.VMEM((ep_count, 8, rows), f32),
            dma((chips,)), dma((chips,)), dma((2, half)), dma((2, half)),
        ],
        compiler_params=pltpu.CompilerParams(
            collective_id=0, has_side_effects=True, vmem_limit_bytes=63 * 1024 * 1024),
    )(*first, both, gains, w_gate, w_up, w_down)
    if inside:
        return result
    return lax.all_to_all(result, "tp", split_axis=1, concat_axis=0, tiled=True)


def solution(mesh):
    return jax.shard_map(
        per_device,
        mesh=mesh,
        in_specs=(
            P("ep", "tp"),
            P("ep", "tp"),
            P("tp", "ep"),
            P(),
            P(),
            P("ep", None),
            P("ep", None),
            P("ep", None, None),
            P("ep", None, None),
            P("ep", None, None),
        ),
        out_specs=P("ep", "tp"),
        check_vma=False,
    )
```

```python
import functools

import jax
import jax.numpy as jnp
from jax import lax
from jax.experimental import pallas as pl
from jax.experimental.pallas import tpu as pltpu
from jax.sharding import PartitionSpec as P

EXPERTS = 40
EPSILON = 1e-05
CHUNKS = 4
MESH = pl.DeviceIdType.MESH


def chip_at(place, chips):
    far = place // (chips // 2)
    return (1 - far) * (2 * place) + far * (2 * (chips - 1 - place) + 1)


def place_of(chip, chips):
    odd = chip % 2
    return (1 - odd) * (chip // 2) + odd * (chips - 1 - chip // 2)


def layer_kernel(
    tp_count, chips, rows, width, local, cap, topk, inside,
    *refs,
):
    if inside:
        attn_ref, resid_ref, w_part, *refs = refs
    else:
        parts_ref, own_ref, *refs = refs
    split_out = inside
    (routed_ref, gain_mix, gain_out, gate_hbm, up_hbm, down_hbm, out_ref, *refs) = refs
    if inside:
        parts_ref, w_all, w_pair_send, w_pair_recv, w_send, w_recv, *refs = refs
    (
    tokens, sums, away, from_pair, from_prev, from_next, hidden, part_in, w_gate, w_up, w_down,
    picked, pick_mats, scaled, finished,
    weight_sem, part_send, part_recv, right_send, right_recv, left_send, left_recv,
    pair_send, pair_recv, down_send, down_recv, back_send, back_recv, cross_send, cross_recv,
    out_send, out_recv,
    routed, places, shares, r_pair_send, r_pair_recv, r_send, r_recv, early_send, early_recv,
    ) = refs
    gain_refs = (gain_mix, gain_out)
    half = chips // 2
    step_rows = rows // CHUNKS
    mid = width // 2
    ep = lax.axis_index("ep")
    tp = lax.axis_index("tp")
    core = ep % 2
    place = place_of(ep // 2, chips)
    after = chip_at((place + 1) % chips, chips) * 2 + core
    before = chip_at((place + chips - 1) % chips, chips) * 2 + core
    pair = ep + 1 - 2 * core

    barrier = pltpu.get_barrier_semaphore()
    for other in (after, before, pair):
        pl.semaphore_signal(barrier, inc=1, device_id={"ep": other}, device_id_type=MESH)
    for k in range(1, tp_count):
        pl.semaphore_signal(barrier, inc=1, device_id={"tp": (tp + k) % tp_count}, device_id_type=MESH)
    pl.semaphore_wait(barrier, 3 + tp_count - 1)

    loads = [
        pltpu.make_async_copy(src, dst, weight_sem.at[i])
        for i, (src, dst) in enumerate(((gate_hbm, w_gate), (up_hbm, w_up), (down_hbm, w_down)))
    ]

    def to_ep(src, dst, send, recv, other):
        return pltpu.make_async_remote_copy(
            src_ref=src, dst_ref=dst, send_sem=send, recv_sem=recv,
            device_id={"ep": other}, device_id_type=MESH)

    def to_tp(src, dst, send, recv, k):
        return pltpu.make_async_remote_copy(
            src_ref=src, dst_ref=dst, send_sem=send, recv_sem=recv,
            device_id={"tp": (tp + k) % tp_count}, device_id_type=MESH)

    def band(c):
        return pl.ds(c * step_rows, step_rows)

    def part_copy(k, c):
        return to_tp(parts_ref.at[k - 1 if inside else (tp + k) % tp_count, band(c)], part_in.at[k - 1, band(c)],
                     part_send.at[k - 1, c], part_recv.at[k - 1, c], k)

    def device_at(back, which=0):
        return chip_at((place + chips + back) % chips, chips) * 2 + (core + which - 2 * core * which)

    def routes_ring(t, way):
        held = routed.at[device_at(-way * (t - 1))]
        return to_ep(held, routed.at[device_at(-way * (t - 1))],
                     r_send.at[(1 - way) // 2, t - 1], r_recv.at[(1 - way) // 2, t - 1],
                     after if way == 1 else before)

    def routes_got(t, way):
        held = routed.at[device_at(-way * t)]
        return to_ep(held, held, r_send.at[(1 - way) // 2, t - 1], r_recv.at[(1 - way) // 2, t - 1],
                     after if way == 1 else before)

    def routes_pair(s, which):
        held = routed.at[device_at(-s, which)]
        return to_ep(held, held, r_pair_send.at[s], r_pair_recv.at[s], pair)

    if inside:
        columns = w_part.shape[0]

        def w_rows(device, t, way):
            if t < half:
                return w_all.at[pl.ds(device * columns, columns)]
            part = columns // 2
            return w_all.at[pl.ds(device * columns + (0 if way == 1 else part), part)]

        def w_ring(t, way, got=0):
            held = w_rows(device_at(-way * (t - 1 + got)), t, way)
            return to_ep(held, held, w_send.at[(1 - way) // 2, t - 1], w_recv.at[(1 - way) // 2, t - 1],
                         after if way == 1 else before)

        def w_pair(s, which):
            held = w_all.at[pl.ds(device_at(-s, which) * columns, columns)]
            return to_ep(held, held, w_pair_send.at[s], w_pair_recv.at[s], pair)

        w_all[pl.ds(ep * columns, columns), :] = w_part[...]
    routed[ep] = routed_ref[...]
    for t in range(1, half + 1):
        for way in (1, -1):
            if t > 1 and inside:
                w_ring(t - 1, way, 1).wait_recv()
            if inside:
                w_ring(t, way).start()
        if inside:
            if t == 1:
                w_pair(0, 0).start()
            else:
                w_pair(t - 1, 0).start()
                w_pair(chips - t + 1, 0).start()
        for way in (1, -1):
            if t > 1:
                routes_got(t - 1, way).wait_recv()
            if t < half or way == 1:
                routes_ring(t, way).start()
        if t == 1:
            routes_pair(0, 0).start()
        else:
            routes_pair(t - 1, 0).start()
            routes_pair(chips - t + 1, 0).start()
    if inside:
        w_ring(half, 1, 1).wait_recv()
        w_ring(half, -1, 1).wait_recv()
        w_pair(half, 0).start()
    routes_got(half, 1).wait_recv()
    routes_pair(half, 0).start()
    if inside:
        for s in range(chips):
            w_pair(s, 1).wait_recv()

        part_width = width // tp_count
        mine = pl.ds(pl.multiple_of(tp * part_width, 128), part_width)

        def project(k, c):
            first = ((tp + k) % tp_count) * rows + c * step_rows
            from_rows = pl.ds(pl.multiple_of(first, step_rows), step_rows)
            hidden[band(c), :] = lax.dot_general(
                attn_ref[from_rows, :], w_all[...], (((1,), (1,)), ((), ())),
                preferred_element_type=jnp.float32)
            hidden[band(c), mine] = hidden[band(c), mine] + resid_ref[from_rows, :].astype(jnp.float32)

        for k in range(1, tp_count):
            for c in range(CHUNKS):
                project(k, c)
                parts_ref[k - 1, band(c), :] = hidden[band(c), :].astype(jnp.bfloat16)
                part_copy(k, c).start()
        for c in range(CHUNKS):
            project(0, c)
    else:
        for c in range(CHUNKS):
            for k in range(1, tp_count):
                part_copy(k, c).start()
    for load in loads:
        load.start()
    def right_copy(t, c):
        return to_ep(tokens.at[t - 1, 0, band(c)], tokens.at[t, 0, band(c)],
                     right_send.at[t - 1, c], right_recv.at[t - 1, c], after)

    def left_copy(t, c):
        return to_ep(tokens.at[(chips - t + 1) % chips, 0, band(c)], tokens.at[chips - t, 0, band(c)],
                     left_send.at[t - 1, c], left_recv.at[t - 1, c], before)

    def right_last(c):
        return to_ep(tokens.at[half - 1, 0, band(c), pl.ds(0, mid)], tokens.at[half, 0, band(c), pl.ds(0, mid)],
                     right_send.at[half - 1, c], right_recv.at[half - 1, c], after)

    def left_last(c):
        return to_ep(tokens.at[half + 1, 0, band(c), pl.ds(mid, mid)], tokens.at[half, 0, band(c), pl.ds(mid, mid)],
                     left_send.at[half - 1, c], left_recv.at[half - 1, c], before)

    def pair_copy(s, c):
        return to_ep(tokens.at[s, 0, band(c)], tokens.at[s, 1, band(c)],
                     pair_send.at[s, c], pair_recv.at[s, c], pair)

    small = min(32, step_rows)

    def norm_rows(at, which, add):
        value = add(at)
        scale = lax.rsqrt(jnp.mean(value * value, axis=1, keepdims=True) + EPSILON)
        return value, (value * scale * gain_refs[which][...][None, :]).astype(jnp.bfloat16)

    for c in range(CHUNKS):
        for k in range(1, tp_count):
            part_copy(k, c).wait_recv()

        def mix(i, carry):
            at = pl.ds(pl.multiple_of(c * step_rows + i * small, small), small)

            def add(at):
                value = (hidden if inside else own_ref)[at, :]
                for k in range(1, tp_count):
                    value = value + part_in[k - 1, at, :].astype(jnp.float32)
                return value

            value, normed = norm_rows(at, 0, add)
            hidden[at, :] = value
            tokens[0, 0, at, :] = normed
            return carry

        lax.fori_loop(0, step_rows // small, mix, 0)
        right_copy(1, c).start()
        left_copy(1, c).start()
        pair_copy(0, c).start()
    for s in range(chips):
        routes_pair(s, 1).wait_recv()

    earlier = jnp.where(
        lax.broadcasted_iota(jnp.int32, (rows, rows), 0) < lax.broadcasted_iota(jnp.int32, (rows, rows), 1),
        1.0, 0.0).astype(jnp.bfloat16)

    def lay_out(block, carry):
        names = routed[block, pl.ds(0, topk), :]
        weights = routed[block, pl.ds(topk, topk), :]
        hits = []
        for f in range(local):
            slot = ep * local + f
            expert = jnp.where(slot < EXPERTS, slot, -1).astype(jnp.float32)
            named = names == expert
            hits.append(jnp.max(jnp.where(named, 1.0, 0.0), axis=0, keepdims=True))
            shares[block, pl.ds(f, 1), :] = jnp.sum(jnp.where(named, weights, 0.0), axis=0, keepdims=True)
        hits = hits + [jnp.zeros((1, rows), jnp.float32)] * (8 - local)
        hits = jnp.concatenate(hits, axis=0)
        rank = jnp.dot(hits.astype(jnp.bfloat16), earlier, preferred_element_type=jnp.float32)
        places[block] = jnp.where(hits > 0.5, rank, -1.0)
        return carry

    lax.fori_loop(0, 2 * chips, lay_out, 0)

    for load in loads:
        load.wait()

    def experts(blocks):
        where = []
        for slot, which, _ in blocks:
            chip = chip_at((place + chips - slot) % chips, chips)
            where.append(chip * 2 + (core + which - 2 * core * which))
        count = len(blocks)

        def one(f, carry):
            at = pl.ds(pl.multiple_of(f * cap, cap), cap)
            columns = []
            for b, (slot, which, _) in enumerate(blocks):
                place_row = places[where[b], pl.ds(f, 1), :]
                gate_row = shares[where[b], pl.ds(f, 1), :]
                index = lax.broadcasted_iota(jnp.int32, (cap, rows), 0).astype(jnp.float32)
                hit = index == place_row
                columns.append(jnp.sum(jnp.where(hit, gate_row, 0.0), axis=1, keepdims=True))
                choose = jnp.where(hit, 1.0, 0.0).astype(jnp.bfloat16)
                pick_mats[b, at, :] = choose
                picked[pl.ds(b * cap, cap), :] = jnp.dot(
                    choose, tokens[slot, which], preferred_element_type=jnp.float32).astype(jnp.bfloat16)
            rows_in = picked[pl.ds(0, count * cap), :]
            gate = jnp.dot(rows_in, w_gate[f], preferred_element_type=jnp.float32)
            up = jnp.dot(rows_in, w_up[f], preferred_element_type=jnp.float32)
            act = (gate / (1.0 + jnp.exp(-gate)) * up).astype(jnp.bfloat16)
            result = jnp.dot(act, w_down[f], preferred_element_type=jnp.float32)
            for b in range(count):
                scaled[b, at, :] = (result[b * cap:(b + 1) * cap, :] * columns[b]).astype(jnp.bfloat16)
            return carry

        lax.fori_loop(0, local, one, 0)
        for b, (_, _, target) in enumerate(blocks):
            target[...] = lax.dot_general(
                pick_mats[b], scaled[b], (((0,), (0,)), ((), ())),
                preferred_element_type=jnp.float32).astype(jnp.bfloat16)

    def cross_copy(s, buffer):
        return to_ep(away.at[buffer], from_pair.at[s], cross_send.at[s], cross_recv.at[s], pair)

    def step(t, carry):
        for c in range(CHUNKS):
            right_copy(t, c).wait_recv()

            @pl.when(t < half - 1)
            def _():
                right_copy(t + 1, c).start()

            @pl.when(t == half - 1)
            def _():
                right_last(c).start()

            pair_copy(t, c).start()
            left_copy(t, c).wait_recv()

            @pl.when(t < half - 1)
            def _():
                left_copy(t + 1, c).start()

            @pl.when(t == half - 1)
            def _():
                left_last(c).start()

            pair_copy(chips - t, c).start()
        for c in range(CHUNKS):
            pair_copy(t, c).wait_recv()
            pair_copy(chips - t, c).wait_recv()
        turn = t % 2

        @pl.when(t > 2)
        def _():
            cross_copy(t - 2, 2 * turn).wait_send()
            cross_copy(chips - t + 2, 2 * turn + 1).wait_send()

        experts([
            (t, 0, sums.at[t]), (t, 1, away.at[2 * turn]),
            (chips - t, 0, sums.at[chips - t]), (chips - t, 1, away.at[2 * turn + 1]),
        ])
        cross_copy(t, 2 * turn).start()
        cross_copy(chips - t, 2 * turn + 1).start()
        return carry

    lax.fori_loop(1, half, step, 0)

    def add_rows(s, at, extra, columns=slice(None)):
        def body(i, carry):
            here = pl.ds(pl.multiple_of(at + i * small, small), small)
            value = sums[s, here, columns].astype(jnp.float32) + from_pair[s, here, columns].astype(jnp.float32)
            if extra is not None:
                value = value + extra[here, columns].astype(jnp.float32)
            sums[s, here, columns] = value.astype(jnp.bfloat16)
            return carry

        lax.fori_loop(0, step_rows // small, body, 0)

    def down_first(c):
        return to_ep(sums.at[half, band(c), pl.ds(0, mid)], from_prev.at[half - 1, band(c), pl.ds(0, mid)],
                     down_send.at[half - 1, c], down_recv.at[half - 1, c], after)

    def back_first(c):
        return to_ep(sums.at[half, band(c), pl.ds(mid, mid)], from_next.at[half - 1, band(c), pl.ds(mid, mid)],
                     back_send.at[half - 1, c], back_recv.at[half - 1, c], before)

    def down_copy(t, c):
        return to_ep(sums.at[chips - t, band(c)], from_prev.at[t - 1, band(c)],
                     down_send.at[t - 1, c], down_recv.at[t - 1, c], after)

    def back_copy(t, c):
        return to_ep(sums.at[t, band(c)], from_next.at[t - 1, band(c)],
                     back_send.at[t - 1, c], back_recv.at[t - 1, c], before)

    last = half - 1

    def down_late(c):
        return to_ep(sums.at[chips - last, band(c), pl.ds(0, mid)], from_prev.at[last - 1, band(c), pl.ds(0, mid)],
                     down_send.at[last - 1, c], down_recv.at[last - 1, c], after)

    def back_late(c):
        return to_ep(sums.at[last, band(c), pl.ds(mid, mid)], from_next.at[last - 1, band(c), pl.ds(mid, mid)],
                     back_send.at[last - 1, c], back_recv.at[last - 1, c], before)

    def down_early(c):
        return to_ep(sums.at[chips - last, band(c), pl.ds(mid, mid)], from_prev.at[last - 1, band(c), pl.ds(mid, mid)],
                     early_send.at[0, c], early_recv.at[0, c], after)

    def back_early(c):
        return to_ep(sums.at[last, band(c), pl.ds(0, mid)], from_next.at[last - 1, band(c), pl.ds(0, mid)],
                     early_send.at[1, c], early_recv.at[1, c], before)

    cross_copy(last, 0).wait_recv()
    cross_copy(chips - last, 0).wait_recv()
    for c in range(CHUNKS):
        add_rows(chips - last, c * step_rows, None, pl.ds(mid, mid))
        down_early(c).start()
        add_rows(last, c * step_rows, None, pl.ds(0, mid))
        back_early(c).start()

    for c in range(CHUNKS):
        right_last(c).wait_recv()
        left_last(c).wait_recv()
        pair_copy(half, c).start()
    for c in range(CHUNKS):
        pair_copy(half, c).wait_recv()
    turn_a, turn_b = half % 2, (half - 1) % 2
    if half > 2:
        cross_copy(half - 2, 2 * turn_a).wait_send()
        cross_copy(chips - half + 2, 2 * turn_a + 1).wait_send()
    experts([(half, 0, sums.at[half]), (half, 1, away.at[2 * turn_a])])
    cross_copy(half, 2 * turn_a).start()

    cross_copy(half, 2 * turn_a).wait_recv()
    for c in range(CHUNKS):
        add_rows(half, c * step_rows, None)
        down_first(c).start()
        back_first(c).start()

    for c in range(CHUNKS):
        pair_copy(0, c).wait_recv()
    cross_copy(half - 1, 2 * turn_b).wait_send()
    cross_copy(chips - half + 1, 2 * turn_b + 1).wait_send()
    experts([(0, 0, sums.at[0]), (0, 1, away.at[2 * turn_b])])
    cross_copy(0, 2 * turn_b).start()

    for c in range(CHUNKS):
        down_first(c).wait_recv()
        add_rows(chips - last, c * step_rows, from_prev.at[last], pl.ds(0, mid))
        down_late(c).start()
        back_first(c).wait_recv()
        add_rows(last, c * step_rows, from_next.at[last], pl.ds(mid, mid))
        back_late(c).start()

    def halves_in(c):
        down_early(c).wait_recv()
        back_early(c).wait_recv()
        down_late(c).wait_recv()
        back_late(c).wait_recv()

    def sum_step(i, carry):
        t = half - 2 - i
        cross_copy(t, 0).wait_recv()
        cross_copy(chips - t, 0).wait_recv()
        for c in range(CHUNKS):
            @pl.when(i == 0)
            def _():
                halves_in(c)

            @pl.when(i > 0)
            def _():
                down_copy(t + 1, c).wait_recv()

            add_rows(chips - t, c * step_rows, from_prev.at[t])
            down_copy(t, c).start()

            @pl.when(i > 0)
            def _():
                back_copy(t + 1, c).wait_recv()

            add_rows(t, c * step_rows, from_next.at[t])
            back_copy(t, c).start()
        return carry

    lax.fori_loop(0, half - 2, sum_step, 0)
    cross_copy(0, 0).wait_recv()

    part_width = width // tp_count

    def out_copy(k, c):
        at = pl.ds(tp * rows + c * step_rows, step_rows)
        return to_tp(finished.at[(tp + k) % tp_count, band(c)], out_ref.at[at],
                     out_send.at[k - 1, c], out_recv.at[k - 1, c], k)

    for c in range(CHUNKS):
        if last == 1:
            halves_in(c)
        else:
            down_copy(1, c).wait_recv()
            back_copy(1, c).wait_recv()

        def close(i, carry):
            at = pl.ds(pl.multiple_of(c * step_rows + i * small, small), small)

            def add(at):
                value = hidden[at, :]
                for part in (sums.at[0], from_pair.at[0], from_prev.at[0], from_next.at[0]):
                    value = value + part[at, :].astype(jnp.float32)
                return value

            _, done = norm_rows(at, 1, add)
            if split_out:
                for r in range(tp_count):
                    finished[r, at, :] = done[:, r * part_width:(r + 1) * part_width]
            else:
                out_ref[at, :] = done
            return carry

        lax.fori_loop(0, step_rows // small, close, 0)
        if split_out:
            for k in range(1, tp_count):
                out_copy(k, c).start()

            def keep(i, carry):
                at = pl.multiple_of(c * step_rows + i * small, small)
                out_ref[pl.ds(tp * rows + at, small), :] = finished[tp, pl.ds(at, small), :]
                return carry

            lax.fori_loop(0, step_rows // small, keep, 0)

    for c in range(CHUNKS):
        for k in range(1, tp_count):
            part_copy(k, c).wait_send()
            if split_out:
                out_copy(k, c).wait_send()
                out_copy(k, c).wait_recv()
        right_last(c).wait_send()
        left_last(c).wait_send()
        down_first(c).wait_send()
        back_first(c).wait_send()
        for copy in (down_early, back_early, down_late, back_late):
            copy(c).wait_send()

    def drain(i, carry):
        t = i + 1
        for c in range(CHUNKS):
            right_copy(t, c).wait_send()
            left_copy(t, c).wait_send()
        return carry

    lax.fori_loop(0, half - 1, drain, 0)

    def drain_sums(i, carry):
        t = i + 1
        for c in range(CHUNKS):
            down_copy(t, c).wait_send()
            back_copy(t, c).wait_send()
        return carry

    lax.fori_loop(0, half - 2, drain_sums, 0)

    def drain_pair(s, carry):
        for c in range(CHUNKS):
            pair_copy(s, c).wait_send()
        return carry

    lax.fori_loop(0, chips, drain_pair, 0)
    cross_copy(half, 2 * turn_a).wait_send()
    cross_copy(0, 2 * turn_b).wait_send()
    for t in range(1, half + 1):
        for way in (1, -1):
            if t < half or way == 1:
                routes_ring(t, way).wait_send()
            if inside:
                w_ring(t, way).wait_send()
    for s in range(chips):
        routes_pair(s, 0).wait_send()
        if inside:
            w_pair(s, 0).wait_send()


def per_device(attn, resid, w_out, gain_mix, gain_out, routes, gates, w_gate, w_up, w_down):
    tp_count = lax.axis_size("tp")
    tp_rank = lax.axis_index("tp")
    ep_count = lax.axis_size("ep")
    tok_dev, width_part = attn.shape
    width = width_part * tp_count
    rows = tok_dev // tp_count
    topk = routes.shape[1]
    local, _, hidden_units = w_gate.shape
    cap = rows * topk // 32
    chips = ep_count // 2
    half = chips // 2

    my_routes = lax.dynamic_slice_in_dim(routes, tp_rank * rows, rows, 0)
    my_gates = lax.dynamic_slice_in_dim(gates, tp_rank * rows, rows, 0)
    both = jnp.concatenate([my_routes.T.astype(jnp.float32), my_gates.T], axis=0)
    inside = width_part % 128 == 0 and w_out.shape[1] % 32 == 0
    if inside:
        first = (attn, resid, w_out.T)
    else:
        columns = lax.all_gather(w_out, "ep", axis=1, tiled=True)
        part = jnp.dot(attn, columns, preferred_element_type=jnp.float32)
        spread = lax.dynamic_update_slice(
            jnp.zeros((tok_dev, width), resid.dtype), resid, (0, tp_rank * width_part))
        part = part + spread.astype(jnp.float32)
        own = lax.dynamic_slice_in_dim(part, tp_rank * rows, rows, 0)
        first = (part.astype(jnp.bfloat16).reshape(tp_count, rows, width), own)

    bf16, f32 = jnp.bfloat16, jnp.float32
    vmem = pl.BlockSpec(memory_space=pltpu.VMEM)
    anywhere = pl.BlockSpec(memory_space=pl.ANY)
    dma = pltpu.SemaphoreType.DMA
    others = tp_count - 1
    out_shape = (tok_dev, width_part) if inside else (rows, width)
    result = pl.pallas_call(
        functools.partial(layer_kernel, tp_count, chips, rows, width, local, cap, topk, inside),
        out_shape=jax.ShapeDtypeStruct(out_shape, bf16),
        in_specs=[vmem] * (len(first) + 3) + [anywhere] * 3,
        out_specs=vmem,
        scratch_shapes=([
            pltpu.VMEM((others, rows, width), bf16),
            pltpu.VMEM((width, width_part), bf16),
            dma((chips,)), dma((chips,)), dma((2, half)), dma((2, half)),
        ] if inside else []) + [
            pltpu.VMEM((chips, 2, rows, width), bf16),
            pltpu.VMEM((chips, rows, width), bf16),
            pltpu.VMEM((4, rows, width), bf16),
            pltpu.VMEM((chips, rows, width), bf16),
            pltpu.VMEM((half, rows, width), bf16),
            pltpu.VMEM((half, rows, width), bf16),
            pltpu.VMEM((rows, width), f32),
            pltpu.VMEM((others, rows, width), bf16),
            pltpu.VMEM(w_gate.shape, bf16),
            pltpu.VMEM(w_up.shape, bf16),
            pltpu.VMEM(w_down.shape, bf16),
            pltpu.VMEM((4 * cap, width), bf16),
            pltpu.VMEM((4, local * cap, rows), bf16),
            pltpu.VMEM((4, local * cap, width), bf16),
            pltpu.VMEM((tp_count, rows, width_part), bf16),
            dma((3,)),
            dma((others, CHUNKS)), dma((others, CHUNKS)),
            dma((half, CHUNKS)), dma((half, CHUNKS)),
            dma((half, CHUNKS)), dma((half, CHUNKS)),
            dma((chips, CHUNKS)), dma((chips, CHUNKS)),
            dma((half, CHUNKS)), dma((half, CHUNKS)),
            dma((half, CHUNKS)), dma((half, CHUNKS)),
            dma((chips,)), dma((chips,)),
            dma((others, CHUNKS)), dma((others, CHUNKS)),
            pltpu.VMEM((ep_count, 2 * topk, rows), f32),
            pltpu.VMEM((ep_count, 8, rows), f32),
            pltpu.VMEM((ep_count, 8, rows), f32),
            dma((chips,)), dma((chips,)), dma((2, half)), dma((2, half)),
            dma((2, CHUNKS)), dma((2, CHUNKS)),
        ],
        compiler_params=pltpu.CompilerParams(
            collective_id=0, has_side_effects=True, vmem_limit_bytes=63 * 1024 * 1024),
    )(*first, both, gain_mix, gain_out, w_gate, w_up, w_down)
    if inside:
        return result
    return lax.all_to_all(result, "tp", split_axis=1, concat_axis=0, tiled=True)


def solution(mesh):
    return jax.shard_map(
        per_device,
        mesh=mesh,
        in_specs=(
            P("ep", "tp"),
            P("ep", "tp"),
            P("tp", "ep"),
            P(),
            P(),
            P("ep", None),
            P("ep", None),
            P("ep", None, None),
            P("ep", None, None),
            P("ep", None, None),
        ),
        out_specs=P("ep", "tp"),
        check_vma=False,
    )
```
